32 devices in a mesh: section: 2 (over x), ep: 16 (over z, y, core).
Axes of the slice: x: 2, y: 2, z: 4, core: 2. Of those that a mesh axis runs over, the one named last changes fastest.
Arguments:
- hidden_in: bfloat16 [2, 128, 4096], P('section', 'ep'), may hold values from -6 to 6
- query: bfloat16 [2, 2, 128, 8192], P('section', None, 'ep'), may hold values from -60 to 60
- new_kv: bfloat16 [2, 2, 128, 1024], P('section', None, 'ep'), may hold values from -4 to 4
- kv_cache: bfloat16 [2, 2, 128, 128, 1024], P('section', None, 'ep'), may hold values from -4 to 4
- lengths: int32 [2, 128], P(None, 'ep'), may hold values from 2 to 128, as said below
- out_proj: bfloat16 [2, 8192, 4096], P('section', 'ep'), may hold values from -0.25 to 0.25
- norm_gain: float32 [2, 4096], P('section'), may hold values from 0.1 to 1.9
- w_gate_up: bfloat16 [2, 16, 4096, 1536], P('section', 'ep'), may hold values from -0.09375 to 0.09375
- w_down: bfloat16 [2, 16, 768, 4096], P('section', 'ep'), may hold values from -0.21875 to 0.21875
- expert_ids: int32 [2, 2, 128, 8], P('section'), may hold values from 0 to 15, all different within a row; in each aligned block of 8 rows (0 to 7, 8 to 15, ..., all dimensions but the last counted through in order) at most 8 rows name the same one
- route_weight: float32 [2, 2, 128, 8], P('section', None, 'ep'), may hold values from 0.05 to 1
Outputs:
- finished: bfloat16 [2, 128, 4096], P('section', 'ep')
The draws below stay inside these ranges and needn't reach their ends.
Inputs may be any that keep to these rules, and one draw needn't show every extreme that they name: `expert_ids`: each row names 8 different experts; among the rows of one index of ep of one micro-batch no expert is named by more than 8 rows, and that bound is reached. `lengths`: row 0 of micro-batch 0 uses all 128 positions.
All inputs are finite; a program needn't handle non-finite values.
Results may differ from the reference program's by a relative error of at most 0.0075.
Values may be sent and summed in bfloat16 or wider, within the bound.
A program may use at most 128 MiB of HBM per device.

```python
import math
import jax
import jax.numpy as jnp
import numpy as np
from jax import lax

D = 4096
HEADS = 64
KVH = 4
HD = 128
FF = 768
TOPK = 8
ROWS_DEV = 8
CACHE = 128
LAYERS = 2
MICRO = 2
ROWS = 128
EXPERTS = 16
CAP = 8
N_EP = 16


def query_and_cache(key):
    key_query = jax.random.fold_in(key, 11)
    key_cache = jax.random.fold_in(key, 12)
    query_shape = (LAYERS, MICRO, ROWS, HEADS * HD)
    cache_shape = (LAYERS, MICRO, ROWS, CACHE, 2 * KVH * HD)
    query = jnp.clip(2.5 * jax.random.normal(key_query, query_shape, jnp.float32), -15.0, 15.0)
    cache = jnp.clip(jax.random.normal(key_cache, cache_shape, jnp.float32), -4.0, 4.0)
    return (query, cache)


def draw_query(key, part):
    return query_and_cache(key)[0].astype(jnp.bfloat16)


def draw_kv_cache(key, part):
    return query_and_cache(key)[1].astype(jnp.bfloat16)


def draw_lengths(key, part):
    key_top = jax.random.fold_in(key, 21)
    key_each = jax.random.fold_in(key, 22)
    blocks = ROWS // ROWS_DEV
    upper = jax.random.randint(key_top, (MICRO, blocks, 1), CACHE // 4, CACHE + 1)
    raw = jax.random.randint(key_each, (MICRO, blocks, ROWS_DEV), 0, 1048576)
    spans = 2 + raw % (upper - 1)
    spans = spans.reshape(MICRO, ROWS)
    return spans.at[0, 0].set(CACHE)


def shard_levels(key, shape, cuts, low, top_value):
    level, own = 1.0, jax.random.fold_in(key, 6)
    for axis_at, parts in cuts:
        steps = jnp.exp(jax.random.uniform(jax.random.fold_in(own, axis_at), (parts,), jnp.float32, low / len(cuts), top_value / len(cuts)))
        level = level * jnp.repeat(steps, shape[axis_at] // parts).reshape([-1 if axis == axis_at else 1 for axis in range(len(shape))])
    return level


def deal_out(key, own, number, rows, count, top, reach, slope):
    sequence = jax.random.permutation(key, count)
    crowded, common = load_shares(count, rows * top, reach, slope, True), load_shares(count, rows * top, reach, slope, False)
    places = jnp.arange(count)

    def named(sizes, turn):
        used = int((sizes > 0).sum())
        fixed = max(1, used // 4)
        passed = fixed + (places - fixed + turn * (used - fixed)) % max(1, count - fixed)
        return jnp.zeros((count,), jnp.int32).at[sequence[jnp.where(places < fixed, places, passed)]].set(jnp.asarray(sizes, jnp.int32))

    sizes = jnp.where(number % 4 == 0, named(crowded, number // 4), named(common, number - number // 4 - 1))
    mixed = jax.random.permutation(jax.random.fold_in(own, 3), count)
    source_of, taker = mixed[0:count // 2 * 2:2], mixed[1:count // 2 * 2:2]
    slack = jnp.minimum(sizes[source_of] - 1, reach - sizes[taker]) // 2
    slack = jnp.where((source_of == sequence[0]) | (taker == sequence[0]) | (sizes[taker] == 0), 0, jnp.maximum(slack, 0))
    passed = jax.random.randint(jax.random.fold_in(own, 4), (count // 2,), 0, 1 << 20) % (slack + 1)
    sizes = sizes.at[source_of].add(-passed).at[taker].add(passed)
    items = jnp.searchsorted(jnp.cumsum(sizes), jnp.arange(rows * top), side="right").astype(jnp.int32)
    grid = items.reshape(top, rows).T
    grid = grid[jax.random.permutation(jax.random.fold_in(own, 1), rows)]
    turn = jax.random.randint(jax.random.fold_in(own, 2), (rows, 1), 0, top)
    return jnp.take_along_axis(grid, (jnp.arange(top)[None, :] + turn) % top, axis=1)


def load_shares(number_of, total, most, slope, full):
    loads = [(1 << 20) // math.isqrt(grade ** slope) + 1 for grade in range(1, number_of + 1)]
    largest = most if full else min(most, max(-(-total // number_of), total * loads[0] // sum(loads)))
    least = 1 if total - largest >= number_of - 1 else 0
    counts, spare = [largest] + [least] * (number_of - 1), total - largest - least * (number_of - 1)
    while spare > 0:
        free = [i for i in range(1, number_of) if counts[i] < largest] or [i for i in range(1, number_of) if counts[i] < most]
        whole, left = sum([loads[i] for i in free]), spare
        for i in free:
            more = min(most - counts[i], max(1, left * loads[i] // whole), spare)
            counts[i] = counts[i] + more
            spare = spare - more
    return np.array(counts)


def normal_values(rng, shape, spread, most, shards=(), held_as=jnp.bfloat16):
    level = shard_levels(rng, shape, shards, -0.22, 0.18) if shards else 1.0
    drawn = jax.random.normal(rng, shape, jnp.float32) * spread * level
    return jnp.minimum(jnp.maximum(drawn, -most), most).astype(held_as)


def setup_inputs(seed: int = 0) -> dict:
    seeds = jax.random.split(jax.random.key(seed), 12)
    hidden_in = normal_values(seeds[0], (MICRO, ROWS, D), 1.0, 6.0, ((0, 2), (1, 16)))
    query = draw_query(jax.random.fold_in(seeds[11], 71), 0)
    new_kv = normal_values(seeds[2], (LAYERS, MICRO, ROWS, 2 * KVH * HD), 1.0, 4.0, ((0, 2), (2, 16)))
    kv_cache = draw_kv_cache(jax.random.fold_in(seeds[11], 71), 0)
    lengths = draw_lengths(jax.random.fold_in(seeds[11], 71), 0)
    out_proj = normal_values(seeds[5], (LAYERS, HEADS * HD, D), (4 * HD) ** -0.5, 0.25, ((0, 2), (1, 16)))
    norm_gain = jnp.clip(1.0 + 0.18 * jax.random.normal(seeds[6], (LAYERS, D), jnp.float32), 0.1, 1.9)
    w_gate_up = normal_values(seeds[7], (LAYERS, EXPERTS, D, 2 * FF), D ** -0.5, 0.09375, ((0, 2), (1, 16)))
    w_down = normal_values(seeds[8], (LAYERS, EXPERTS, FF, D), FF ** -0.5, 0.21875, ((0, 2), (1, 16)))
    expert_ids_keys = jax.random.split(jax.random.fold_in(seeds[9], 1), LAYERS * MICRO * ROWS // ROWS_DEV)
    expert_ids_turns = jax.random.permutation(jax.random.fold_in(seeds[9], 3), LAYERS * MICRO * ROWS // ROWS_DEV)
    expert_ids = jax.vmap(lambda own, number: deal_out(jax.random.fold_in(seeds[9], 2), own, number, ROWS_DEV, EXPERTS, TOPK, CAP, 2))(expert_ids_keys, expert_ids_turns).reshape((LAYERS, MICRO, ROWS, TOPK))
    route_weight = jnp.clip(jnp.exp(math.log(1.0) - 2.9957323 * jax.random.uniform(seeds[10], (LAYERS, MICRO, ROWS, TOPK), jnp.float32) ** shard_levels(seeds[10], (LAYERS, MICRO, ROWS, TOPK), ((0, 2), (2, 16)), -0.2, 0.2)), 0.05, 1.0)
    return dict(hidden_in=hidden_in, query=query, new_kv=new_kv, kv_cache=kv_cache, lengths=lengths, out_proj=out_proj, norm_gain=norm_gain, w_gate_up=w_gate_up, w_down=w_down, expert_ids=expert_ids, route_weight=route_weight)


def slot_numbers(picks, count):
    flat = picks.reshape(picks.shape[:-2] + (-1,))
    onehot = (flat[..., None] == jnp.arange(count, dtype=jnp.int32)).astype(jnp.int32)
    earlier = jnp.cumsum(onehot, axis=-2) - onehot
    return lax.optimization_barrier(jnp.sum(onehot * earlier, axis=-1)).reshape(picks.shape)

def attend(query, cache, newest, lengths):
    group = HEADS // KVH
    scale = 1.0 / math.sqrt(HD)
    q_heads = query.astype(jnp.float32).reshape(ROWS, KVH, group, HD)
    keys = cache[..., :KVH * HD].astype(jnp.float32).reshape(ROWS, CACHE, KVH, HD)
    values = cache[..., KVH * HD:].astype(jnp.float32).reshape(ROWS, CACHE, KVH, HD)
    new_keys = newest[:, :KVH * HD].astype(jnp.float32).reshape(ROWS, KVH, HD)
    new_values = newest[:, KVH * HD:].astype(jnp.float32).reshape(ROWS, KVH, HD)
    scores = jnp.einsum('rgqd,rpgd->rgqp', q_heads, keys) * scale
    fresh = jnp.einsum('rgqd,rgd->rgq', q_heads, new_keys) * scale
    valid = (jnp.arange(CACHE, dtype=jnp.int32)[None, :] < lengths[:, None])[:, None, None, :]
    top = jnp.maximum(lax.optimization_barrier(jnp.max(jnp.where(valid, scores, -jnp.inf), axis=-1)), fresh)
    expo = jnp.where(valid, jnp.exp(scores - top[..., None]), 0.0)
    expo_new = jnp.exp(fresh - top)
    total = lax.optimization_barrier(jnp.sum(expo, axis=-1)) + expo_new
    probs = lax.optimization_barrier((expo / total[..., None]).astype(jnp.bfloat16)).astype(jnp.float32)
    probs_new = lax.optimization_barrier((expo_new / total).astype(jnp.bfloat16)).astype(jnp.float32)
    mixed = jnp.einsum('rgqp,rpgd->rgqd', probs, values) + probs_new[..., None] * new_values[:, :, None, :]
    return mixed.reshape(ROWS, HEADS * HD).astype(jnp.bfloat16)

def experts_apply(x_rows, picks, weights, w_pair, w_out):
    slots = slot_numbers(picks.reshape(N_EP, ROWS_DEV, TOPK), EXPERTS).reshape(ROWS, TOPK)
    share = weights / lax.optimization_barrier(jnp.sum(weights, axis=-1, keepdims=True))
    source = jnp.arange(ROWS, dtype=jnp.int32) // ROWS_DEV
    position = source[:, None] * CAP + slots
    cells = jnp.arange(N_EP * CAP, dtype=jnp.int32)

    def one_expert(total, item):
        pair, down, index = item
        hit = picks == index
        chosen = hit[:, :, None] & (position[:, :, None] == cells[None, None, :])
        select = jnp.transpose(jnp.any(chosen, axis=1)).astype(jnp.bfloat16)
        buffer = jnp.dot(select, x_rows, preferred_element_type=jnp.float32).astype(jnp.bfloat16)
        act = jnp.dot(buffer, pair, preferred_element_type=jnp.float32)
        units = (jax.nn.silu(act[:, :FF]) * act[:, FF:]).astype(jnp.bfloat16)
        output = jnp.dot(units, down, preferred_element_type=jnp.float32).astype(jnp.bfloat16)
        mixing = lax.optimization_barrier(jnp.sum(jnp.where(chosen, share[:, :, None], 0.0), axis=1))
        total = total + jnp.dot(mixing, output.astype(jnp.float32), precision=lax.Precision.HIGHEST)
        return (total, None)
    start = jnp.zeros((ROWS, D), jnp.float32)
    total, _ = lax.scan(one_expert, start, (w_pair, w_out, jnp.arange(EXPERTS, dtype=jnp.int32)))
    return total

def layer_apply(hidden, layer, micro, query, new_kv, kv_cache, lengths, out_proj, norm_gain, w_gate_up, w_down, expert_ids, route_weight):
    attn = attend(query[layer, micro], kv_cache[layer, micro], new_kv[layer, micro], lengths[micro])
    h_att = hidden.astype(jnp.float32) + jnp.dot(attn, out_proj[layer], preferred_element_type=jnp.float32)
    meansq = lax.optimization_barrier(jnp.mean(h_att * h_att, axis=-1, keepdims=True))
    x_rows = (h_att * lax.rsqrt(meansq + 1e-06) * norm_gain[layer][None, :]).astype(jnp.bfloat16)
    moe = experts_apply(x_rows, expert_ids[layer, micro], route_weight[layer, micro], w_gate_up[layer], w_down[layer])
    return (h_att + moe).astype(jnp.bfloat16)

def reference(hidden_in, query, new_kv, kv_cache, lengths, out_proj, norm_gain, w_gate_up, w_down, expert_ids, route_weight):
    results = [None] * MICRO
    for micro in range(MICRO):
        hidden = hidden_in[micro]
        for tick in range(LAYERS):
            layer = (micro + tick) % LAYERS
            hidden = layer_apply(hidden, layer, micro, query, new_kv, kv_cache, lengths, out_proj, norm_gain, w_gate_up, w_down, expert_ids, route_weight)
        results[(micro + MICRO - 1) % MICRO] = hidden
    return jnp.stack(results)
```

```python
import functools
import math

import jax
import jax.numpy as jnp
from jax import lax
from jax.experimental import pallas as pl
from jax.experimental.pallas import tpu as pltpu
from jax.sharding import PartitionSpec as P

HEADS = 64
KVH = 4
HD = 128
STEP_ROWS = 4
TILE = 512
UNIT_TILE = 256
MESH = pl.DeviceIdType.MESH


def attend_kernel(order_ref, len_ref, q_ref, new_ref, kv_ref, out_ref):
    group = HEADS // KVH
    scale = 1.0 / math.sqrt(HD)
    micro = order_ref[pl.program_id(0)]
    first = pl.program_id(1) * STEP_ROWS
    for row in range(STEP_ROWS):
        q = q_ref[0, row]
        newest = new_ref[0, row].astype(jnp.float32)
        span = len_ref[micro, first + row]
        scores = (
            jnp.concatenate(
                [
                    lax.dot_general(
                        q[g * group : (g + 1) * group],
                        kv_ref[0, row, :, g * HD : (g + 1) * HD],
                        (((1,), (1,)), ((), ())),
                        preferred_element_type=jnp.float32,
                    )
                    for g in range(KVH)
                ],
                axis=0,
            )
            * scale
        )
        new_keys = jnp.concatenate(
            [jnp.broadcast_to(newest[g : g + 1], (group, HD)) for g in range(KVH)], axis=0
        )
        new_values = jnp.concatenate(
            [jnp.broadcast_to(newest[KVH + g : KVH + g + 1], (group, HD)) for g in range(KVH)],
            axis=0,
        )
        fresh = jnp.sum(q.astype(jnp.float32) * new_keys, axis=-1, keepdims=True) * scale
        valid = lax.broadcasted_iota(jnp.int32, scores.shape, 1) < span
        top = jnp.maximum(
            jnp.max(jnp.where(valid, scores, -jnp.inf), axis=-1, keepdims=True), fresh
        )
        expo = jnp.where(valid, jnp.exp(scores - top), 0.0)
        expo_new = jnp.exp(fresh - top)
        total = jnp.sum(expo, axis=-1, keepdims=True) + expo_new
        probs = (expo / total).astype(jnp.bfloat16)
        probs_new = (expo_new / total).astype(jnp.bfloat16).astype(jnp.float32)
        mixed = jnp.concatenate(
            [
                jnp.dot(
                    probs[g * group : (g + 1) * group],
                    kv_ref[0, row, :, (KVH + g) * HD : (KVH + g + 1) * HD],
                    preferred_element_type=jnp.float32,
                )
                for g in range(KVH)
            ],
            axis=0,
        )
        out_ref[0, row] = (mixed + probs_new * new_values).astype(jnp.bfloat16)


def attend_all(order, lengths, query, newest, cache):
    micros, rows = query.shape[:2]
    positions = cache.shape[2]
    q = query.reshape(micros, rows, HEADS, HD)
    new = newest.reshape(micros, rows, 2 * KVH, HD)

    def taken(*rest):
        return lambda t, i, order, spans: (order[t], i) + rest

    return pl.pallas_call(
        attend_kernel,
        out_shape=jax.ShapeDtypeStruct((micros, rows, HEADS, HD), jnp.bfloat16),
        grid_spec=pltpu.PrefetchScalarGridSpec(
            num_scalar_prefetch=2,
            grid=(micros, rows // STEP_ROWS),
            in_specs=[
                pl.BlockSpec((1, STEP_ROWS, HEADS, HD), taken(0, 0)),
                pl.BlockSpec((1, STEP_ROWS, 2 * KVH, HD), taken(0, 0)),
                pl.BlockSpec((1, STEP_ROWS, positions, 2 * KVH * HD), taken(0, 0)),
            ],
            out_specs=pl.BlockSpec(
                (1, STEP_ROWS, HEADS, HD), lambda t, i, order, spans: (t, i, 0, 0)
            ),
        ),
        compiler_params=pltpu.CompilerParams(vmem_limit_bytes=16 << 20),
    )(order, lengths, q, new, cache)


def folded(rows):
    half = rows.shape[1] // 2
    return jnp.concatenate([rows[:, :half], rows[:, half:]], axis=0).astype(jnp.bfloat16)


def unfolded(block):
    wide = block.astype(jnp.float32)
    half = wide.shape[0] // 2
    return jnp.concatenate([wide[:half], wide[half:]], axis=1)


def layers_kernel(n, sections, a_ref, share_ref, hidden_ref, gain_ref, wo_hbm, wgu_hbm, wd_hbm, out_ref, *scratch):
    levels = n.bit_length() - 1
    (wo, wgu, wd, a_all, share_all, x_all, units, x_out, x_in, h_out, h_in) = scratch[:11]
    rest = scratch[11:]
    acc = rest[:2]
    sent = (rest[2 : 2 + levels], rest[2 + levels : 2 + 2 * levels])
    got = (rest[2 + 2 * levels : 2 + 3 * levels], rest[2 + 3 * levels : 2 + 4 * levels])
    (w_sem, own_sem, a_send, a_recv, s_send, s_recv, r_send, r_recv, g_send, g_recv, h_send, h_recv) = rest[2 + 4 * levels :]

    me = lax.axis_index("ep")
    stage = lax.axis_index("section")
    rows = hidden_ref.shape[0]
    width = hidden_ref.shape[1]
    cols = a_all.shape[2]
    bits = [(me // (1 << j)) % 2 for j in range(levels)]

    def flipped(j):
        return me + (1 - 2 * bits[j]) * (1 << j)

    place = sum(bits[j] * (1 << (levels - 1 - j)) for j in range(levels))

    loads = [
        pltpu.make_async_copy(src, dst, w_sem.at[i])
        for i, (src, dst) in enumerate(((wo_hbm, wo), (wgu_hbm, wgu), (wd_hbm, wd)))
    ]
    for load in loads:
        load.start()

    barrier = pltpu.get_barrier_semaphore()

    @pl.loop(1, n)
    def _(d):
        pl.semaphore_signal(
            barrier, inc=1, device_id={"ep": lax.rem(me + d, n)}, device_id_type=MESH
        )

    for d in range(1, sections):
        pl.semaphore_signal(
            barrier,
            inc=1,
            device_id={"section": lax.rem(stage + d, sections)},
            device_id_type=MESH,
        )
    pl.semaphore_wait(barrier, n - 1 + sections - 1)

    def a_part(peer):
        return a_ref.at[:, pl.ds(pl.multiple_of(peer * cols, cols), cols)]

    def exchange(d):
        peer = lax.rem(me + d, n)
        return (
            pltpu.make_async_remote_copy(
                src_ref=a_part(peer),
                dst_ref=a_all.at[place],
                send_sem=a_send.at[d],
                recv_sem=a_recv.at[d],
                device_id={"ep": peer},
                device_id_type=MESH,
            ),
            pltpu.make_async_remote_copy(
                src_ref=share_ref.at[peer],
                dst_ref=share_all.at[place],
                send_sem=s_send.at[d],
                recv_sem=s_recv.at[d],
                device_id={"ep": peer},
                device_id_type=MESH,
            ),
        )

    @pl.loop(1, n)
    def _(d):
        for copy in exchange(d):
            copy.start()

    own = (
        pltpu.make_async_copy(a_part(me), a_all.at[place], own_sem.at[0]),
        pltpu.make_async_copy(share_ref.at[me], share_all.at[place], own_sem.at[1]),
    )
    for copy in own:
        copy.start()
    for copy in own:
        copy.wait()

    @pl.loop(1, n)
    def _(d):
        for copy in exchange(d):
            copy.wait()

    core = bits[0] == 1
    half = n * rows // 2

    def keep_and_send(c, partial, at):
        low, high = partial[:half], partial[half:]
        acc[c][:, at] = jnp.where(core, high, low)
        sent[c][0][:, at] = jnp.where(core, low, high).astype(jnp.bfloat16)

    def reduce_copy(c, call, j):
        return pltpu.make_async_remote_copy(
            src_ref=sent[c][j],
            dst_ref=got[c][j],
            send_sem=r_send.at[call, j],
            recv_sem=r_recv.at[call, j],
            device_id={"ep": flipped(j)},
            device_id_type=MESH,
        )

    def advance(c, call, j):
        reduce_copy(c, call, j - 1).wait()
        size = half >> j
        if j < levels - 1:
            keep = pl.ds(pl.multiple_of(bits[j] * size, size), size)
            send = pl.ds(pl.multiple_of((1 - bits[j]) * size, size), size)
            sent[c][j][...] = (
                acc[c][send, :] + got[c][j - 1][send, :].astype(jnp.float32)
            ).astype(jnp.bfloat16)
            reduce_copy(c, call, j).start()
            acc[c][:size, :] = acc[c][keep, :] + got[c][j - 1][keep, :].astype(jnp.float32)
        else:
            both = acc[c][: 2 * size, :] + got[c][j - 1][...].astype(jnp.float32)
            upper = bits[j] == 1
            low, high = both[:size], both[size:]
            sent[c][j][...] = folded(jnp.where(upper, low, high))
            reduce_copy(c, call, j).start()
            acc[c][:size, :] = jnp.where(upper, high, low)

    def total(c, call):
        reduce_copy(c, call, levels - 1).wait()
        return acc[c][:rows, :] + unfolded(got[c][levels - 1][...])

    def gather(tick, x):
        x_out[...] = folded(x)
        copy = pltpu.make_async_remote_copy(
            src_ref=x_out,
            dst_ref=x_in,
            send_sem=g_send.at[tick, levels - 1],
            recv_sem=g_recv.at[tick, levels - 1],
            device_id={"ep": flipped(levels - 1)},
            device_id_type=MESH,
        )
        copy.start()
        copy.wait()
        other = unfolded(x_in[...])
        upper = bits[levels - 1] == 1
        pair = jnp.concatenate([jnp.where(upper, other, x), jnp.where(upper, x, other)], axis=0)
        pair_at = pl.multiple_of((place // 2) * (2 * rows), 2 * rows)
        x_all[pl.ds(pair_at, 2 * rows), :] = pair.astype(jnp.bfloat16)
        for j in range(levels - 2, -1, -1):
            blocks = 1 << (levels - 1 - j)
            size = rows * blocks
            held = x_all.at[pl.ds(pl.multiple_of((place // blocks) * size, size), size)]
            copy = pltpu.make_async_remote_copy(
                src_ref=held,
                dst_ref=held,
                send_sem=g_send.at[tick, j],
                recv_sem=g_recv.at[tick, j],
                device_id={"ep": flipped(j)},
                device_id_type=MESH,
            )
            copy.start()
            copy.wait()

    loads[0].wait()

    @pl.loop(0, width // TILE)
    def _(i):
        at = pl.ds(pl.multiple_of(i * TILE, TILE), TILE)
        product = jnp.dot(
            a_all[...].reshape(n * 2 * rows, cols), wo[:, at], preferred_element_type=jnp.float32
        ).reshape(n, 2 * rows, TILE)
        keep_and_send(0, product[:, :rows].reshape(n * rows, TILE), at)
        keep_and_send(1, product[:, rows:].reshape(n * rows, TILE), at)

    reduce_copy(0, 0, 0).start()
    reduce_copy(1, 1, 0).start()
    for j in range(1, levels):
        advance(0, 0, j)

    hidden = hidden_ref[...].astype(jnp.float32)
    later = list(range(1, levels))
    for tick in range(2):
        h_att = hidden + total(tick, tick)
        meansq = jnp.mean(h_att * h_att, axis=-1, keepdims=True)
        x = h_att * lax.rsqrt(meansq + 1e-06) * gain_ref[...]
        gather(tick, x)
        if tick == 0:
            loads[1].wait()
            if later:
                advance(1, 1, later.pop(0))
        units_wide = units.shape[1]

        @pl.loop(0, units_wide // UNIT_TILE)
        def _(i):
            at = pl.multiple_of(i * UNIT_TILE, UNIT_TILE)
            gate = jnp.dot(
                x_all[...], wgu[:, pl.ds(at, UNIT_TILE)], preferred_element_type=jnp.float32
            )
            up_at = pl.multiple_of(units_wide + i * UNIT_TILE, UNIT_TILE)
            up = jnp.dot(
                x_all[...], wgu[:, pl.ds(up_at, UNIT_TILE)], preferred_element_type=jnp.float32
            )
            units[:, pl.ds(at, UNIT_TILE)] = (gate / (1.0 + jnp.exp(-gate)) * up).astype(
                jnp.bfloat16
            )

        if tick == 0:
            loads[2].wait()
            if later:
                advance(1, 1, later.pop(0))

        share = share_all[:, tick * rows : (tick + 1) * rows, :].reshape(n * rows, 128)[:, :1]

        @pl.loop(0, width // TILE)
        def _(i):
            at = pl.ds(pl.multiple_of(i * TILE, TILE), TILE)
            keep_and_send(
                0, jnp.dot(units[...], wd[:, at], preferred_element_type=jnp.float32) * share, at
            )

        call = 2 + tick
        reduce_copy(0, call, 0).start()
        if tick == 0:
            while later:
                advance(1, 1, later.pop(0))
        for j in range(1, levels):
            advance(0, call, j)
        done = h_att + total(0, call)
        if tick == 0:
            h_out[...] = folded(done)
            copy = pltpu.make_async_remote_copy(
                src_ref=h_out,
                dst_ref=h_in,
                send_sem=h_send,
                recv_sem=h_recv,
                device_id={"section": lax.rem(stage + 1, sections)},
                device_id_type=MESH,
            )
            copy.start()
            copy.wait()
            hidden = unfolded(h_in[...])
        else:
            out_ref[...] = done.astype(jnp.bfloat16)


def layers_all(n, sections, attn, share, hidden, gain, proj_rows, w_pair, w_out):
    levels = n.bit_length() - 1
    rows, width = hidden.shape
    cols = proj_rows.shape[0]
    vmem, dma = pltpu.VMEM, pltpu.SemaphoreType.DMA
    bf16, f32 = jnp.bfloat16, jnp.float32
    folded_shape = (2 * rows, width // 2)
    halves = [vmem((n * rows >> (j + 1), width), bf16) for j in range(levels - 1)]
    halves.append(vmem(folded_shape, bf16))
    return pl.pallas_call(
        functools.partial(layers_kernel, n, sections),
        out_shape=jax.ShapeDtypeStruct((rows, width), bf16),
        in_specs=[pl.BlockSpec(memory_space=pltpu.VMEM)] * 4
        + [pl.BlockSpec(memory_space=pl.ANY)] * 3,
        out_specs=pl.BlockSpec(memory_space=pltpu.VMEM),
        scratch_shapes=[
            vmem(proj_rows.shape, bf16),
            vmem(w_pair.shape, bf16),
            vmem(w_out.shape, bf16),
            vmem((n, 2 * rows, cols), bf16),
            vmem((n, 2 * rows, 128), f32),
            vmem((n * rows, width), bf16),
            vmem((n * rows, w_out.shape[0]), bf16),
            vmem(folded_shape, bf16),
            vmem(folded_shape, bf16),
            vmem(folded_shape, bf16),
            vmem(folded_shape, bf16),
        ]
        + [vmem((n * rows // 2, width), f32)] * 2
        + halves * 4
        + [
            dma((3,)),
            dma((2,)),
            dma((n,)),
            dma((n,)),
            dma((n,)),
            dma((n,)),
            dma((4, levels)),
            dma((4, levels)),
            dma((2, levels)),
            dma((2, levels)),
            dma(()),
            dma(()),
        ],
        compiler_params=pltpu.CompilerParams(
            collective_id=0, has_side_effects=True, vmem_limit_bytes=60 << 20
        ),
        cost_estimate=pl.CostEstimate(
            flops=int(2 * n * rows * width * (2 * cols + 6 * w_out.shape[0])),
            bytes_accessed=int(2 * width * (cols + 3 * w_out.shape[0])),
            transcendentals=0,
        ),
    )(attn, share, hidden, gain, proj_rows, w_pair, w_out)


def on_device(
    n,
    sections,
    hidden_in,
    query,
    new_kv,
    kv_cache,
    lengths,
    out_proj,
    norm_gain,
    w_gate_up,
    w_down,
    expert_ids,
    route_weight,
):
    position = lax.axis_index("section")
    member = lax.axis_index("ep")
    rows = hidden_in.shape[1]
    order = (position - jnp.arange(2, dtype=jnp.int32)) % 2
    attn = attend_all(order, lengths, query[0], new_kv[0], kv_cache[0])
    picks = lax.dynamic_slice_in_dim(expert_ids[0], member * rows, rows, 1)
    weights = route_weight[0]
    share = weights / jnp.sum(weights, axis=-1, keepdims=True)
    swap = position == 1
    picks = jnp.where(swap, picks[::-1], picks).reshape(2 * rows, -1)
    share = jnp.where(swap, share[::-1], share).reshape(2 * rows, -1)
    chosen = picks[None] == jnp.arange(n, dtype=jnp.int32)[:, None, None]
    dense = jnp.sum(jnp.where(chosen, share[None], 0.0), axis=-1)
    return layers_all(
        n,
        sections,
        attn.reshape(2 * rows, HEADS * HD),
        jnp.broadcast_to(dense[:, :, None], (n, 2 * rows, 128)),
        hidden_in[0],
        norm_gain,
        out_proj[0],
        w_gate_up[0, 0],
        w_down[0, 0],
    )[None]


def solution(mesh):
    in_specs = (
        P("section", "ep", None),
        P("section", None, "ep", None),
        P("section", None, "ep", None),
        P("section", None, "ep", None, None),
        P(None, "ep"),
        P("section", "ep", None),
        P("section", None),
        P("section", "ep", None, None),
        P("section", "ep", None, None),
        P("section", None, None, None),
        P("section", None, "ep", None),
    )
    out_specs = P("section", "ep", None)
    return jax.shard_map(
        functools.partial(on_device, mesh.shape["ep"], mesh.shape["section"]),
        mesh=mesh,
        in_specs=in_specs,
        out_specs=out_specs,
        check_vma=False,
    )
```

```python
import functools
import math

import jax
import jax.numpy as jnp
from jax import lax
from jax.experimental import pallas as pl
from jax.experimental.pallas import tpu as pltpu
from jax.sharding import PartitionSpec as P

HEADS = 64
KVH = 4
HD = 128
STEP_ROWS = 4
TILE = 512
UNIT_TILE = 256
MESH = pl.DeviceIdType.MESH


def attend_kernel(order_ref, len_ref, q_ref, new_ref, kv_ref, out_ref):
    group = HEADS // KVH
    scale = 1.0 / math.sqrt(HD)
    micro = order_ref[pl.program_id(0)]
    first = pl.program_id(1) * STEP_ROWS
    for row in range(STEP_ROWS):
        q = q_ref[0, row]
        newest = new_ref[0, row].astype(jnp.float32)
        span = len_ref[micro, first + row]
        scores = (
            jnp.concatenate(
                [
                    lax.dot_general(
                        q[g * group : (g + 1) * group],
                        kv_ref[0, row, :, g * HD : (g + 1) * HD],
                        (((1,), (1,)), ((), ())),
                        preferred_element_type=jnp.float32,
                    )
                    for g in range(KVH)
                ],
                axis=0,
            )
            * scale
        )
        new_keys = jnp.concatenate(
            [jnp.broadcast_to(newest[g : g + 1], (group, HD)) for g in range(KVH)], axis=0
        )
        new_values = jnp.concatenate(
            [jnp.broadcast_to(newest[KVH + g : KVH + g + 1], (group, HD)) for g in range(KVH)],
            axis=0,
        )
        fresh = jnp.sum(q.astype(jnp.float32) * new_keys, axis=-1, keepdims=True) * scale
        valid = lax.broadcasted_iota(jnp.int32, scores.shape, 1) < span
        top = jnp.maximum(
            jnp.max(jnp.where(valid, scores, -jnp.inf), axis=-1, keepdims=True), fresh
        )
        expo = jnp.where(valid, jnp.exp(scores - top), 0.0)
        expo_new = jnp.exp(fresh - top)
        total = jnp.sum(expo, axis=-1, keepdims=True) + expo_new
        probs = (expo / total).astype(jnp.bfloat16)
        probs_new = (expo_new / total).astype(jnp.bfloat16).astype(jnp.float32)
        mixed = jnp.concatenate(
            [
                jnp.dot(
                    probs[g * group : (g + 1) * group],
                    kv_ref[0, row, :, (KVH + g) * HD : (KVH + g + 1) * HD],
                    preferred_element_type=jnp.float32,
                )
                for g in range(KVH)
            ],
            axis=0,
        )
        out_ref[0, row] = (mixed + probs_new * new_values).astype(jnp.bfloat16)


def attend_all(order, lengths, query, newest, cache):
    micros, rows = query.shape[:2]
    positions = cache.shape[2]
    q = query.reshape(micros, rows, HEADS, HD)
    new = newest.reshape(micros, rows, 2 * KVH, HD)

    def taken(*rest):
        return lambda t, i, order, spans: (order[t], i) + rest

    return pl.pallas_call(
        attend_kernel,
        out_shape=jax.ShapeDtypeStruct((micros, rows, HEADS, HD), jnp.bfloat16),
        grid_spec=pltpu.PrefetchScalarGridSpec(
            num_scalar_prefetch=2,
            grid=(micros, rows // STEP_ROWS),
            in_specs=[
                pl.BlockSpec((1, STEP_ROWS, HEADS, HD), taken(0, 0)),
                pl.BlockSpec((1, STEP_ROWS, 2 * KVH, HD), taken(0, 0)),
                pl.BlockSpec((1, STEP_ROWS, positions, 2 * KVH * HD), taken(0, 0)),
            ],
            out_specs=pl.BlockSpec(
                (1, STEP_ROWS, HEADS, HD), lambda t, i, order, spans: (t, i, 0, 0)
            ),
        ),
        compiler_params=pltpu.CompilerParams(vmem_limit_bytes=16 << 20),
    )(order, lengths, q, new, cache)


def folded(rows):
    half = rows.shape[1] // 2
    return jnp.concatenate([rows[:, :half], rows[:, half:]], axis=0).astype(jnp.bfloat16)


def unfolded(block):
    wide = block.astype(jnp.float32)
    half = wide.shape[0] // 2
    return jnp.concatenate([wide[:half], wide[half:]], axis=1)


def layers_kernel(n, sections, a_ref, share_ref, hidden_ref, gain_ref, wo_hbm, wgu_hbm, wd_hbm, out_ref, *scratch):
    levels = n.bit_length() - 1
    (wo, wgu, wd, a_all, share_all, units, h_out, h_in) = scratch[:8]
    x_all, x_out, x_in = scratch[8:10], scratch[10:12], scratch[12:14]
    rest = scratch[14:]
    acc = (rest[:2], rest[2:4])
    rest = rest[4:]
    parts = [rest[i * levels : (i + 1) * levels] for i in range(8)]
    sent = (parts[0:2], parts[2:4])
    got = (parts[4:6], parts[6:8])
    (w_sem, own_sem, a_send, a_recv, s_send, s_recv, r_send, r_recv, g_send, g_recv, h_send, h_recv) = rest[8 * levels :]

    me = lax.axis_index("ep")
    stage = lax.axis_index("section")
    rows = hidden_ref.shape[0]
    width = hidden_ref.shape[1]
    span = width // 2
    cols = a_all.shape[2]
    bits = [(me // (1 << j)) % 2 for j in range(levels)]
    orders = (list(range(levels)), [0] + list(range(2, levels)) + [1])
    places = [
        sum(bits[order[i]] * (1 << (levels - 1 - i)) for i in range(levels)) for order in orders
    ]
    place = places[0]

    def first_place(second):
        owner = sum(
            ((second >> (levels - 1 - i)) & 1) << orders[1][i] for i in range(levels)
        )
        return sum(((owner >> i) & 1) << (levels - 1 - i) for i in range(levels))

    to_first = [first_place(second) for second in range(n)]

    def reordered(value, blocks):
        return jnp.concatenate([value[b * rows : (b + 1) * rows] for b in blocks], axis=0)

    def flipped(j):
        return me + (1 - 2 * bits[j]) * (1 << j)

    loads = [
        pltpu.make_async_copy(src, dst, w_sem.at[i])
        for i, (src, dst) in enumerate(((wo_hbm, wo), (wgu_hbm, wgu), (wd_hbm, wd)))
    ]
    loads[0].start()

    barrier = pltpu.get_barrier_semaphore()

    @pl.loop(1, n)
    def _(d):
        pl.semaphore_signal(
            barrier, inc=1, device_id={"ep": lax.rem(me + d, n)}, device_id_type=MESH
        )

    for d in range(1, sections):
        pl.semaphore_signal(
            barrier,
            inc=1,
            device_id={"section": lax.rem(stage + d, sections)},
            device_id_type=MESH,
        )
    pl.semaphore_wait(barrier, n - 1 + sections - 1)

    def a_part(peer):
        return a_ref.at[:, pl.ds(pl.multiple_of(peer * cols, cols), cols)]

    def exchange(d):
        peer = lax.rem(me + d, n)
        return (
            pltpu.make_async_remote_copy(
                src_ref=a_part(peer),
                dst_ref=a_all.at[place],
                send_sem=a_send.at[d],
                recv_sem=a_recv.at[d],
                device_id={"ep": peer},
                device_id_type=MESH,
            ),
            pltpu.make_async_remote_copy(
                src_ref=share_ref.at[peer],
                dst_ref=share_all.at[place],
                send_sem=s_send.at[d],
                recv_sem=s_recv.at[d],
                device_id={"ep": peer},
                device_id_type=MESH,
            ),
        )

    for which in range(2):

        @pl.loop(1, n)
        def _(d):
            exchange(d)[which].start()

    own = (
        pltpu.make_async_copy(a_part(me), a_all.at[place], own_sem.at[0]),
        pltpu.make_async_copy(share_ref.at[me], share_all.at[place], own_sem.at[1]),
    )
    for copy in own:
        copy.start()
    for copy in own:
        copy.wait()

    @pl.loop(1, n)
    def _(d):
        exchange(d)[0].wait()

    core = bits[0] == 1
    half = n * rows // 2

    def keep_and_send(c, h, partial, at):
        if h == 1:
            partial = reordered(partial, to_first)
        low, high = partial[:half], partial[half:]
        acc[c][h][:, at] = jnp.where(core, high, low)
        sent[c][h][0][:, at] = jnp.where(core, low, high).astype(jnp.bfloat16)

    def reduce_copy(c, call, h, j):
        return pltpu.make_async_remote_copy(
            src_ref=sent[c][h][j],
            dst_ref=got[c][h][j],
            send_sem=r_send.at[2 * call + h, j],
            recv_sem=r_recv.at[2 * call + h, j],
            device_id={"ep": flipped(orders[h][j])},
            device_id_type=MESH,
        )

    def advance(c, call, j):
        size = half >> j
        for h in range(2):
            mine = bits[orders[h][j]]
            sums, before = acc[c][h], got[c][h][j - 1]
            reduce_copy(c, call, h, j - 1).wait()
            if j < levels - 1:
                keep = pl.ds(pl.multiple_of(mine * size, size), size)
                send = pl.ds(pl.multiple_of((1 - mine) * size, size), size)
                sent[c][h][j][...] = (
                    sums[send, :] + before[send, :].astype(jnp.float32)
                ).astype(jnp.bfloat16)
                reduce_copy(c, call, h, j).start()
                sums[:size, :] = sums[keep, :] + before[keep, :].astype(jnp.float32)
            else:
                both = sums[: 2 * size, :] + before[...].astype(jnp.float32)
                upper = mine == 1
                low, high = both[:size], both[size:]
                sent[c][h][j][...] = folded(jnp.where(upper, low, high))
                reduce_copy(c, call, h, j).start()
                sums[:size, :] = jnp.where(upper, high, low)

    def total(c, call):
        sums = []
        for h in range(2):
            reduce_copy(c, call, h, levels - 1).wait()
            sums.append(acc[c][h][:rows, :] + unfolded(got[c][h][levels - 1][...]))
        return jnp.concatenate(sums, axis=1)

    def gather_copy(tick, h, i):
        if i == levels - 1:
            src, dst = x_out[h], x_in[h]
        else:
            blocks = 1 << (levels - 1 - i)
            size = rows * blocks
            at = pl.ds(pl.multiple_of((places[h] // blocks) * size, size), size)
            src = dst = x_all[h].at[at]
        return pltpu.make_async_remote_copy(
            src_ref=src,
            dst_ref=dst,
            send_sem=g_send.at[2 * tick + h, i],
            recv_sem=g_recv.at[2 * tick + h, i],
            device_id={"ep": flipped(orders[h][i])},
            device_id_type=MESH,
        )

    def gather(tick, x):
        for h in range(2):
            x_out[h][...] = folded(x[:, h * span : (h + 1) * span])
            gather_copy(tick, h, levels - 1).start()
        for i in range(levels - 2, -2, -1):
            for h in range(2):
                gather_copy(tick, h, i + 1).wait()
                if i == levels - 2:
                    own_x = x[:, h * span : (h + 1) * span]
                    other = unfolded(x_in[h][...])
                    upper = bits[orders[h][levels - 1]] == 1
                    pair = jnp.concatenate(
                        [jnp.where(upper, other, own_x), jnp.where(upper, own_x, other)], axis=0
                    )
                    pair_at = pl.multiple_of((places[h] // 2) * (2 * rows), 2 * rows)
                    x_all[h][pl.ds(pair_at, 2 * rows), :] = pair.astype(jnp.bfloat16)
                if i >= 0:
                    gather_copy(tick, h, i).start()

    loads[0].wait()
    loads[1].start()
    loads[2].start()
    for h in range(2):

        @pl.loop(0, span // TILE)
        def _(i):
            at = pl.ds(pl.multiple_of(i * TILE, TILE), TILE)
            product = jnp.dot(
                a_all[...].reshape(n * 2 * rows, cols),
                wo[:, pl.ds(pl.multiple_of(h * span + i * TILE, TILE), TILE)],
                preferred_element_type=jnp.float32,
            ).reshape(n, 2 * rows, TILE)
            keep_and_send(0, h, product[:, :rows].reshape(n * rows, TILE), at)
            keep_and_send(1, h, product[:, rows:].reshape(n * rows, TILE), at)

        reduce_copy(0, 0, h, 0).start()

    for j in range(1, levels):
        advance(0, 0, j)
        if j == 1:
            for h in range(2):
                reduce_copy(1, 1, h, 0).start()

    @pl.loop(1, n)
    def _(d):
        exchange(d)[1].wait()

    hidden = hidden_ref[...].astype(jnp.float32)
    later = list(range(1, levels))
    for tick in range(2):
        h_att = hidden + total(tick, tick)
        meansq = jnp.mean(h_att * h_att, axis=-1, keepdims=True)
        x = h_att * lax.rsqrt(meansq + 1e-06) * gain_ref[...]
        gather(tick, x)
        if tick == 0:
            loads[1].wait()
            if later:
                advance(1, 1, later.pop(0))
        units_wide = units.shape[1]

        def pushed(at):
            second = jnp.dot(
                x_all[1][...], wgu[span:, pl.ds(at, UNIT_TILE)], preferred_element_type=jnp.float32
            )
            back = [to_first.index(b) for b in range(n)]
            return jnp.dot(
                x_all[0][...], wgu[:span, pl.ds(at, UNIT_TILE)], preferred_element_type=jnp.float32
            ) + reordered(second, back)

        @pl.loop(0, units_wide // UNIT_TILE)
        def _(i):
            at = pl.multiple_of(i * UNIT_TILE, UNIT_TILE)
            gate = pushed(at)
            up = pushed(pl.multiple_of(units_wide + i * UNIT_TILE, UNIT_TILE))
            units[:, pl.ds(at, UNIT_TILE)] = (gate / (1.0 + jnp.exp(-gate)) * up).astype(
                jnp.bfloat16
            )

        if tick == 0:
            loads[2].wait()
            if later:
                advance(1, 1, later.pop(0))

        share = share_all[:, tick * rows : (tick + 1) * rows, :].reshape(n * rows, 128)[:, :1]
        call = 2 + tick
        for h in range(2):

            @pl.loop(0, span // TILE)
            def _(i):
                at = pl.ds(pl.multiple_of(i * TILE, TILE), TILE)
                down = wd[:, pl.ds(pl.multiple_of(h * span + i * TILE, TILE), TILE)]
                keep_and_send(
                    0,
                    h,
                    jnp.dot(units[...], down, preferred_element_type=jnp.float32) * share,
                    at,
                )

            reduce_copy(0, call, h, 0).start()

        if tick == 0:
            while later:
                advance(1, 1, later.pop(0))
        for j in range(1, levels):
            advance(0, call, j)
        done = h_att + total(0, call)
        if tick == 0:
            h_out[...] = folded(done)
            copy = pltpu.make_async_remote_copy(
                src_ref=h_out,
                dst_ref=h_in,
                send_sem=h_send,
                recv_sem=h_recv,
                device_id={"section": lax.rem(stage + 1, sections)},
                device_id_type=MESH,
            )
            copy.start()
            copy.wait()
            hidden = unfolded(h_in[...])
        else:
            out_ref[...] = done.astype(jnp.bfloat16)


def layers_all(n, sections, attn, share, hidden, gain, proj_rows, w_pair, w_out):
    levels = n.bit_length() - 1
    rows, width = hidden.shape
    cols = proj_rows.shape[0]
    vmem, dma = pltpu.VMEM, pltpu.SemaphoreType.DMA
    bf16, f32 = jnp.bfloat16, jnp.float32
    span = width // 2
    h_shape, x_shape = (2 * rows, span), (2 * rows, span // 2)
    halves = [vmem((n * rows >> (j + 1), span), bf16) for j in range(levels - 1)]
    halves.append(vmem(x_shape, bf16))
    return pl.pallas_call(
        functools.partial(layers_kernel, n, sections),
        out_shape=jax.ShapeDtypeStruct((rows, width), bf16),
        in_specs=[pl.BlockSpec(memory_space=pltpu.VMEM)] * 4
        + [pl.BlockSpec(memory_space=pl.ANY)] * 3,
        out_specs=pl.BlockSpec(memory_space=pltpu.VMEM),
        scratch_shapes=[
            vmem(proj_rows.shape, bf16),
            vmem(w_pair.shape, bf16),
            vmem(w_out.shape, bf16),
            vmem((n, 2 * rows, cols), bf16),
            vmem((n, 2 * rows, 128), f32),
            vmem((n * rows, w_out.shape[0]), bf16),
            vmem(h_shape, bf16),
            vmem(h_shape, bf16),
        ]
        + [vmem((n * rows, span), bf16)] * 2
        + [vmem(x_shape, bf16)] * 4
        + [vmem((n * rows // 2, span), f32)] * 4
        + halves * 8
        + [
            dma((3,)),
            dma((2,)),
            dma((n,)),
            dma((n,)),
            dma((n,)),
            dma((n,)),
            dma((8, levels)),
            dma((8, levels)),
            dma((4, levels)),
            dma((4, levels)),
            dma(()),
            dma(()),
        ],
        compiler_params=pltpu.CompilerParams(
            collective_id=0, has_side_effects=True, vmem_limit_bytes=60 << 20
        ),
        cost_estimate=pl.CostEstimate(
            flops=int(2 * n * rows * width * (2 * cols + 6 * w_out.shape[0])),
            bytes_accessed=int(2 * width * (cols + 3 * w_out.shape[0])),
            transcendentals=0,
        ),
    )(attn, share, hidden, gain, proj_rows, w_pair, w_out)


def on_device(
    n,
    sections,
    hidden_in,
    query,
    new_kv,
    kv_cache,
    lengths,
    out_proj,
    norm_gain,
    w_gate_up,
    w_down,
    expert_ids,
    route_weight,
):
    position = lax.axis_index("section")
    member = lax.axis_index("ep")
    rows = hidden_in.shape[1]
    order = (position - jnp.arange(2, dtype=jnp.int32)) % 2
    attn = attend_all(order, lengths, query[0], new_kv[0], kv_cache[0])
    picks = lax.dynamic_slice_in_dim(expert_ids[0], member * rows, rows, 1)
    weights = route_weight[0]
    share = weights / jnp.sum(weights, axis=-1, keepdims=True)
    swap = position == 1
    picks = jnp.where(swap, picks[::-1], picks).reshape(2 * rows, -1)
    share = jnp.where(swap, share[::-1], share).reshape(2 * rows, -1)
    chosen = picks[None] == jnp.arange(n, dtype=jnp.int32)[:, None, None]
    dense = jnp.sum(jnp.where(chosen, share[None], 0.0), axis=-1)
    return layers_all(
        n,
        sections,
        attn.reshape(2 * rows, HEADS * HD),
        jnp.broadcast_to(dense[:, :, None], (n, 2 * rows, 128)),
        hidden_in[0],
        norm_gain,
        out_proj[0],
        w_gate_up[0, 0],
        w_down[0, 0],
    )[None]


def solution(mesh):
    in_specs = (
        P("section", "ep", None),
        P("section", None, "ep", None),
        P("section", None, "ep", None),
        P("section", None, "ep", None, None),
        P(None, "ep"),
        P("section", "ep", None),
        P("section", None),
        P("section", "ep", None, None),
        P("section", "ep", None, None),
        P("section", None, None, None),
        P("section", None, "ep", None),
    )
    out_specs = P("section", "ep", None)
    return jax.shard_map(
        functools.partial(on_device, mesh.shape["ep"], mesh.shape["section"]),
        mesh=mesh,
        in_specs=in_specs,
        out_specs=out_specs,
        check_vma=False,
    )
```

```python
import functools
import math

import jax
import jax.numpy as jnp
from jax import lax
from jax.experimental import pallas as pl
from jax.experimental.pallas import tpu as pltpu
from jax.sharding import PartitionSpec as P

HEADS = 64
KVH = 4
HD = 128
STEP_ROWS = 4
TILE = 512
UNIT_TILE = 256
MESH = pl.DeviceIdType.MESH


def attend_kernel(order_ref, len_ref, q_ref, new_ref, kv_ref, out_ref):
    group = HEADS // KVH
    scale = 1.0 / math.sqrt(HD)
    micro = order_ref[pl.program_id(0)]
    first = pl.program_id(1) * STEP_ROWS
    for row in range(STEP_ROWS):
        q = q_ref[0, row]
        newest = new_ref[0, row].astype(jnp.float32)
        span = len_ref[micro, first + row]
        scores = (
            jnp.concatenate(
                [
                    lax.dot_general(
                        q[g * group : (g + 1) * group],
                        kv_ref[0, row, :, g * HD : (g + 1) * HD],
                        (((1,), (1,)), ((), ())),
                        preferred_element_type=jnp.float32,
                    )
                    for g in range(KVH)
                ],
                axis=0,
            )
            * scale
        )
        new_keys = jnp.concatenate(
            [jnp.broadcast_to(newest[g : g + 1], (group, HD)) for g in range(KVH)], axis=0
        )
        new_values = jnp.concatenate(
            [jnp.broadcast_to(newest[KVH + g : KVH + g + 1], (group, HD)) for g in range(KVH)],
            axis=0,
        )
        fresh = jnp.sum(q.astype(jnp.float32) * new_keys, axis=-1, keepdims=True) * scale
        valid = lax.broadcasted_iota(jnp.int32, scores.shape, 1) < span
        top = jnp.maximum(
            jnp.max(jnp.where(valid, scores, -jnp.inf), axis=-1, keepdims=True), fresh
        )
        expo = jnp.where(valid, jnp.exp(scores - top), 0.0)
        expo_new = jnp.exp(fresh - top)
        total = jnp.sum(expo, axis=-1, keepdims=True) + expo_new
        probs = (expo / total).astype(jnp.bfloat16)
        probs_new = (expo_new / total).astype(jnp.bfloat16).astype(jnp.float32)
        mixed = jnp.concatenate(
            [
                jnp.dot(
                    probs[g * group : (g + 1) * group],
                    kv_ref[0, row, :, (KVH + g) * HD : (KVH + g + 1) * HD],
                    preferred_element_type=jnp.float32,
                )
                for g in range(KVH)
            ],
            axis=0,
        )
        out_ref[0, row] = (mixed + probs_new * new_values).astype(jnp.bfloat16)


def attend_all(order, lengths, query, newest, cache):
    micros, rows = query.shape[:2]
    positions = cache.shape[2]
    q = query.reshape(micros, rows, HEADS, HD)
    new = newest.reshape(micros, rows, 2 * KVH, HD)

    def taken(*rest):
        return lambda t, i, order, spans: (order[t], i) + rest

    return pl.pallas_call(
        attend_kernel,
        out_shape=jax.ShapeDtypeStruct((micros, rows, HEADS, HD), jnp.bfloat16),
        grid_spec=pltpu.PrefetchScalarGridSpec(
            num_scalar_prefetch=2,
            grid=(micros, rows // STEP_ROWS),
            in_specs=[
                pl.BlockSpec((1, STEP_ROWS, HEADS, HD), taken(0, 0)),
                pl.BlockSpec((1, STEP_ROWS, 2 * KVH, HD), taken(0, 0)),
                pl.BlockSpec((1, STEP_ROWS, positions, 2 * KVH * HD), taken(0, 0)),
            ],
            out_specs=pl.BlockSpec(
                (1, STEP_ROWS, HEADS, HD), lambda t, i, order, spans: (t, i, 0, 0)
            ),
        ),
        compiler_params=pltpu.CompilerParams(vmem_limit_bytes=16 << 20),
    )(order, lengths, q, new, cache)


def folded(rows):
    half = rows.shape[1] // 2
    return jnp.concatenate([rows[:, :half], rows[:, half:]], axis=0).astype(jnp.bfloat16)


def unfolded(block):
    wide = block.astype(jnp.float32)
    half = wide.shape[0] // 2
    return jnp.concatenate([wide[:half], wide[half:]], axis=1)


def layers_kernel(n, sections, a_ref, picks_ref, weights_ref, hidden_ref, gain_ref, wo_hbm, wgu_hbm, wd_hbm, out_ref, *scratch):
    levels = n.bit_length() - 1
    (wo, wgu, wd, a_all, share_ref, share_all, units, h_out, h_in) = scratch[:9]
    x_all, x_out, x_in = scratch[9:11], scratch[11:13], scratch[13:15]
    rest = scratch[15:]
    acc = (rest[:2], rest[2:4])
    rest = rest[4:]
    parts = [rest[i * levels : (i + 1) * levels] for i in range(8)]
    sent = (parts[0:2], parts[2:4])
    got = (parts[4:6], parts[6:8])
    (w_sem, own_sem, a_send, a_recv, s_send, s_recv, r_send, r_recv, g_send, g_recv, h_send, h_recv) = rest[8 * levels :]

    me = lax.axis_index("ep")
    stage = lax.axis_index("section")
    rows = hidden_ref.shape[0]
    width = hidden_ref.shape[1]
    span = width // 2
    cols = a_all.shape[2]
    bits = [(me // (1 << j)) % 2 for j in range(levels)]
    orders = (list(range(levels)), [0, 2, 1] + list(range(3, levels)))
    places = [
        sum(bits[order[i]] * (1 << (levels - 1 - i)) for i in range(levels)) for order in orders
    ]
    place = places[0]

    def first_place(second):
        owner = sum(
            ((second >> (levels - 1 - i)) & 1) << orders[1][i] for i in range(levels)
        )
        return sum(((owner >> i) & 1) << (levels - 1 - i) for i in range(levels))

    to_first = [first_place(second) for second in range(n)]

    def reordered(value, blocks):
        return jnp.concatenate([value[b * rows : (b + 1) * rows] for b in blocks], axis=0)

    def flipped(j):
        return me + (1 - 2 * bits[j]) * (1 << j)

    loads = [
        pltpu.make_async_copy(src, dst, w_sem.at[i])
        for i, (src, dst) in enumerate(((wo_hbm, wo), (wgu_hbm, wgu), (wd_hbm, wd)))
    ]
    loads[0].start()

    barrier = pltpu.get_barrier_semaphore()

    @pl.loop(1, n)
    def _(d):
        pl.semaphore_signal(
            barrier, inc=1, device_id={"ep": lax.rem(me + d, n)}, device_id_type=MESH
        )

    for d in range(1, sections):
        pl.semaphore_signal(
            barrier,
            inc=1,
            device_id={"section": lax.rem(stage + d, sections)},
            device_id_type=MESH,
        )
    pl.semaphore_wait(barrier, n - 1 + sections - 1)

    def a_part(peer):
        return a_ref.at[:, pl.ds(pl.multiple_of(peer * cols, cols), cols)]

    def exchange(d):
        peer = lax.rem(me + d, n)
        return (
            pltpu.make_async_remote_copy(
                src_ref=a_part(peer),
                dst_ref=a_all.at[place],
                send_sem=a_send.at[d],
                recv_sem=a_recv.at[d],
                device_id={"ep": peer},
                device_id_type=MESH,
            ),
            pltpu.make_async_remote_copy(
                src_ref=share_ref.at[peer],
                dst_ref=share_all.at[place],
                send_sem=s_send.at[d],
                recv_sem=s_recv.at[d],
                device_id={"ep": peer},
                device_id_type=MESH,
            ),
        )

    @pl.loop(1, n)
    def _(d):
        exchange(d)[0].start()

    own = (
        pltpu.make_async_copy(a_part(me), a_all.at[place], own_sem.at[0]),
        pltpu.make_async_copy(share_ref.at[me], share_all.at[place], own_sem.at[1]),
    )
    own[0].start()
    weights = weights_ref[...]
    shares = weights / jnp.sum(weights, axis=-1, keepdims=True)
    for expert in range(n):
        named = jnp.where(picks_ref[...] == expert, shares, 0.0)
        share_ref[expert] = jnp.broadcast_to(
            jnp.sum(named, axis=-1, keepdims=True), share_ref.shape[1:]
        )

    @pl.loop(1, n)
    def _(d):
        exchange(d)[1].start()

    own[1].start()
    for copy in own:
        copy.wait()

    @pl.loop(1, n)
    def _(d):
        exchange(d)[0].wait()

    core = bits[0] == 1
    half = n * rows // 2

    def keep_and_send(c, h, partial, at):
        if h == 1:
            partial = reordered(partial, to_first)
        low, high = partial[:half], partial[half:]
        acc[c][h][:, at] = jnp.where(core, high, low)
        sent[c][h][0][:, at] = jnp.where(core, low, high).astype(jnp.bfloat16)

    def reduce_copy(c, call, h, j):
        return pltpu.make_async_remote_copy(
            src_ref=sent[c][h][j],
            dst_ref=got[c][h][j],
            send_sem=r_send.at[2 * call + h, j],
            recv_sem=r_recv.at[2 * call + h, j],
            device_id={"ep": flipped(orders[h][j])},
            device_id_type=MESH,
        )

    def advance(c, call, j):
        size = half >> j
        for h in range(2):
            mine = bits[orders[h][j]]
            sums, before = acc[c][h], got[c][h][j - 1]
            reduce_copy(c, call, h, j - 1).wait()
            if j < levels - 1:
                keep = pl.ds(pl.multiple_of(mine * size, size), size)
                send = pl.ds(pl.multiple_of((1 - mine) * size, size), size)
                sent[c][h][j][...] = (
                    sums[send, :] + before[send, :].astype(jnp.float32)
                ).astype(jnp.bfloat16)
                reduce_copy(c, call, h, j).start()
                sums[:size, :] = sums[keep, :] + before[keep, :].astype(jnp.float32)
            else:
                both = sums[: 2 * size, :] + before[...].astype(jnp.float32)
                upper = mine == 1
                low, high = both[:size], both[size:]
                sent[c][h][j][...] = folded(jnp.where(upper, low, high))
                reduce_copy(c, call, h, j).start()
                sums[:size, :] = jnp.where(upper, high, low)

    def total(c, call):
        sums = []
        for h in range(2):
            reduce_copy(c, call, h, levels - 1).wait()
            sums.append(acc[c][h][:rows, :] + unfolded(got[c][h][levels - 1][...]))
        return jnp.concatenate(sums, axis=1)

    def gather_copy(tick, h, i):
        if i == levels - 1:
            src, dst = x_out[h], x_in[h]
        else:
            blocks = 1 << (levels - 1 - i)
            size = rows * blocks
            at = pl.ds(pl.multiple_of((places[h] // blocks) * size, size), size)
            src = dst = x_all[h].at[at]
        return pltpu.make_async_remote_copy(
            src_ref=src,
            dst_ref=dst,
            send_sem=g_send.at[2 * tick + h, i],
            recv_sem=g_recv.at[2 * tick + h, i],
            device_id={"ep": flipped(orders[h][i])},
            device_id_type=MESH,
        )

    def gather(tick, x):
        for h in range(2):
            x_out[h][...] = folded(x[:, h * span : (h + 1) * span])
            gather_copy(tick, h, levels - 1).start()
        for i in range(levels - 2, -2, -1):
            for h in range(2):
                gather_copy(tick, h, i + 1).wait()
                if i == levels - 2:
                    own_x = x[:, h * span : (h + 1) * span]
                    other = unfolded(x_in[h][...])
                    upper = bits[orders[h][levels - 1]] == 1
                    pair = jnp.concatenate(
                        [jnp.where(upper, other, own_x), jnp.where(upper, own_x, other)], axis=0
                    )
                    pair_at = pl.multiple_of((places[h] // 2) * (2 * rows), 2 * rows)
                    x_all[h][pl.ds(pair_at, 2 * rows), :] = pair.astype(jnp.bfloat16)
                if i >= 0:
                    gather_copy(tick, h, i).start()

    loads[0].wait()
    loads[1].start()
    loads[2].start()
    for h in range(2):

        @pl.loop(0, span // TILE)
        def _(i):
            at = pl.ds(pl.multiple_of(i * TILE, TILE), TILE)
            product = jnp.dot(
                a_all[...].reshape(n * 2 * rows, cols),
                wo[:, pl.ds(pl.multiple_of(h * span + i * TILE, TILE), TILE)],
                preferred_element_type=jnp.float32,
            ).reshape(n, 2 * rows, TILE)
            keep_and_send(0, h, product[:, :rows].reshape(n * rows, TILE), at)
            keep_and_send(1, h, product[:, rows:].reshape(n * rows, TILE), at)

        reduce_copy(0, 0, h, 0).start()

    for j in range(1, levels):
        advance(0, 0, j)
        if j == 1:
            for h in range(2):
                reduce_copy(1, 1, h, 0).start()

    @pl.loop(1, n)
    def _(d):
        exchange(d)[1].wait()

    hidden = hidden_ref[...].astype(jnp.float32)
    later = list(range(1, levels))
    for tick in range(2):
        h_att = hidden + total(tick, tick)
        meansq = jnp.mean(h_att * h_att, axis=-1, keepdims=True)
        x = h_att * lax.rsqrt(meansq + 1e-06) * gain_ref[...]
        gather(tick, x)
        if tick == 0:
            loads[1].wait()
            if later:
                advance(1, 1, later.pop(0))
        units_wide = units.shape[1]

        def pushed(at):
            second = jnp.dot(
                x_all[1][...], wgu[span:, pl.ds(at, UNIT_TILE)], preferred_element_type=jnp.float32
            )
            back = [to_first.index(b) for b in range(n)]
            return jnp.dot(
                x_all[0][...], wgu[:span, pl.ds(at, UNIT_TILE)], preferred_element_type=jnp.float32
            ) + reordered(second, back)

        @pl.loop(0, units_wide // UNIT_TILE)
        def _(i):
            at = pl.multiple_of(i * UNIT_TILE, UNIT_TILE)
            gate = pushed(at)
            up = pushed(pl.multiple_of(units_wide + i * UNIT_TILE, UNIT_TILE))
            units[:, pl.ds(at, UNIT_TILE)] = (gate / (1.0 + jnp.exp(-gate)) * up).astype(
                jnp.bfloat16
            )

        if tick == 0:
            loads[2].wait()
            if later:
                advance(1, 1, later.pop(0))

        share = share_all[:, tick * rows : (tick + 1) * rows, :].reshape(n * rows, 128)[:, :1]
        call = 2 + tick
        for h in range(2):

            @pl.loop(0, span // TILE)
            def _(i):
                at = pl.ds(pl.multiple_of(i * TILE, TILE), TILE)
                down = wd[:, pl.ds(pl.multiple_of(h * span + i * TILE, TILE), TILE)]
                keep_and_send(
                    0,
                    h,
                    jnp.dot(units[...], down, preferred_element_type=jnp.float32) * share,
                    at,
                )

            reduce_copy(0, call, h, 0).start()

        if tick == 0:
            while later:
                advance(1, 1, later.pop(0))
        for j in range(1, levels):
            advance(0, call, j)
        done = h_att + total(0, call)
        if tick == 0:
            h_out[...] = folded(done)
            copy = pltpu.make_async_remote_copy(
                src_ref=h_out,
                dst_ref=h_in,
                send_sem=h_send,
                recv_sem=h_recv,
                device_id={"section": lax.rem(stage + 1, sections)},
                device_id_type=MESH,
            )
            copy.start()
            copy.wait()
            hidden = unfolded(h_in[...])
        else:
            out_ref[...] = done.astype(jnp.bfloat16)


def layers_all(n, sections, attn, picks, weights, hidden, gain, proj_rows, w_pair, w_out):
    levels = n.bit_length() - 1
    rows, width = hidden.shape
    cols = proj_rows.shape[0]
    vmem, dma = pltpu.VMEM, pltpu.SemaphoreType.DMA
    bf16, f32 = jnp.bfloat16, jnp.float32
    span = width // 2
    h_shape, x_shape = (2 * rows, span), (2 * rows, span // 2)
    halves = [vmem((n * rows >> (j + 1), span), bf16) for j in range(levels - 1)]
    halves.append(vmem(x_shape, bf16))
    return pl.pallas_call(
        functools.partial(layers_kernel, n, sections),
        out_shape=jax.ShapeDtypeStruct((rows, width), bf16),
        in_specs=[pl.BlockSpec(memory_space=pltpu.VMEM)] * 5
        + [pl.BlockSpec(memory_space=pl.ANY)] * 3,
        out_specs=pl.BlockSpec(memory_space=pltpu.VMEM),
        scratch_shapes=[
            vmem(proj_rows.shape, bf16),
            vmem(w_pair.shape, bf16),
            vmem(w_out.shape, bf16),
            vmem((n, 2 * rows, cols), bf16),
            vmem((n, 2 * rows, 128), f32),
            vmem((n, 2 * rows, 128), f32),
            vmem((n * rows, w_out.shape[0]), bf16),
            vmem(h_shape, bf16),
            vmem(h_shape, bf16),
        ]
        + [vmem((n * rows, span), bf16)] * 2
        + [vmem(x_shape, bf16)] * 4
        + [vmem((n * rows // 2, span), f32)] * 4
        + halves * 8
        + [
            dma((3,)),
            dma((2,)),
            dma((n,)),
            dma((n,)),
            dma((n,)),
            dma((n,)),
            dma((8, levels)),
            dma((8, levels)),
            dma((4, levels)),
            dma((4, levels)),
            dma(()),
            dma(()),
        ],
        compiler_params=pltpu.CompilerParams(
            collective_id=0, has_side_effects=True, vmem_limit_bytes=60 << 20
        ),
        cost_estimate=pl.CostEstimate(
            flops=int(2 * n * rows * width * (2 * cols + 6 * w_out.shape[0])),
            bytes_accessed=int(2 * width * (cols + 3 * w_out.shape[0])),
            transcendentals=0,
        ),
    )(attn, picks, weights, hidden, gain, proj_rows, w_pair, w_out)


def on_device(
    n,
    sections,
    hidden_in,
    query,
    new_kv,
    kv_cache,
    lengths,
    out_proj,
    norm_gain,
    w_gate_up,
    w_down,
    expert_ids,
    route_weight,
):
    position = lax.axis_index("section")
    member = lax.axis_index("ep")
    rows = hidden_in.shape[1]
    order = (position - jnp.arange(2, dtype=jnp.int32)) % 2
    attn = attend_all(order, lengths, query[0], new_kv[0], kv_cache[0])
    picks = lax.dynamic_slice_in_dim(expert_ids[0], member * rows, rows, 1)
    weights = route_weight[0]
    swap = position == 1
    picks = jnp.where(swap, picks[::-1], picks).reshape(2 * rows, -1)
    weights = jnp.where(swap, weights[::-1], weights).reshape(2 * rows, -1)
    return layers_all(
        n,
        sections,
        attn.reshape(2 * rows, HEADS * HD),
        picks,
        weights,
        hidden_in[0],
        norm_gain,
        out_proj[0],
        w_gate_up[0, 0],
        w_down[0, 0],
    )[None]


def solution(mesh):
    in_specs = (
        P("section", "ep", None),
        P("section", None, "ep", None),
        P("section", None, "ep", None),
        P("section", None, "ep", None, None),
        P(None, "ep"),
        P("section", "ep", None),
        P("section", None),
        P("section", "ep", None, None),
        P("section", "ep", None, None),
        P("section", None, None, None),
        P("section", None, "ep", None),
    )
    out_specs = P("section", "ep", None)
    return jax.shard_map(
        functools.partial(on_device, mesh.shape["ep"], mesh.shape["section"]),
        mesh=mesh,
        in_specs=in_specs,
        out_specs=out_specs,
        check_vma=False,
    )
```
